512 devices in a mesh: seq: 64 (over y, z), head: 8 (over x, core).
Axes of the slice: x: 4, y: 4, z: 16, core: 2. Of those that a mesh axis runs over, the one named last changes fastest.
Arguments:
- queries: bfloat16 [1024, 4096], P('seq', 'head'), may hold values from -9 to 9
- keys: bfloat16 [8, 131072, 128], P('head', 'seq'), may hold values from -9 to 9
- values: bfloat16 [8, 131072, 128], P('head', 'seq'), may hold values from -6 to 6
- mask: int32 [8, 1024], P(None, 'seq'), may hold values from 0 to 1, as said below
- out_proj: bfloat16 [4096, 4096], P('head', 'seq'), may hold values from -0.09375 to 0.09375
Outputs:
- output: bfloat16 [1024, 4096], P('seq', 'head')
The draws below stay inside these ranges and needn't reach their ends.
Inputs may be any that keep to these rules, and one draw needn't show every extreme that they name: `mask`: each entry is 0 or 1; the share of ones differs strongly between the cached positions of different seq shards.
All inputs are finite; a program needn't handle non-finite values.
Results may differ from the reference program's by a relative error of at most 0.0057.
Values may be sent and summed in bfloat16 or wider, within the bound.
A program may use at most 64 MiB of HBM per device.

```python
import jax
import jax.numpy as jnp
from jax import lax

D = 4096
HD = 128
GROUP = 4
KVH = 8
QH = 32
QROWS = 1024
CACHE_DEV = 2048
KEYS = 131072
BLK = 128


def draw_mask(key, part):
    key_blocks = KEYS // BLK
    per_shard = CACHE_DEV // BLK
    shard_count = key_blocks // per_shard
    first, second = jax.random.split(jax.random.fold_in(key, 17))
    offset = jax.random.randint(second, (), 0, shard_count)
    shard = jnp.arange(key_blocks, dtype=jnp.int32) // per_shard
    level = (shard * 29 + offset) % shard_count
    threshold = 150 + 800 * level // max(shard_count - 1, 1)
    draws = jax.random.randint(first, (QROWS // BLK, key_blocks), 0, 1000)
    return (draws < threshold[None, :]).astype(jnp.int32)


def block_levels(key, dims, cuts, low, largest):
    def one(position, blocks):
        steps = jax.random.uniform(jax.random.fold_in(jax.random.fold_in(key, 6), position), (blocks,), jnp.float32, low / len(cuts), largest / len(cuts))
        return jnp.repeat(jnp.exp(steps), dims[position] // blocks).reshape((-1,) + (1,) * (len(dims) - position - 1))

    gain = one(*cuts[0])
    for cut in cuts[1:]:
        gain = gain * one(*cut)
    return gain


def gaussian(stream_key, dims, scale, limit, cuts=(), kind=jnp.bfloat16):
    array = scale * jax.random.normal(stream_key, dims, jnp.float32)
    if cuts:
        array = array * block_levels(stream_key, dims, cuts, -0.22, 0.18)
    return jnp.clip(array, -limit, limit).astype(kind)


def setup_inputs(seed: int = 0) -> dict:
    arg_keys = jax.random.split(jax.random.key(seed), 6)
    return {
        "queries": gaussian(arg_keys[0], (QROWS, QH * HD), 1.6, 9.0, ((0, 64), (1, 8))),
        "keys": gaussian(arg_keys[1], (KVH, KEYS, HD), 1.6, 9.0, ((0, 8), (1, 64))),
        "values": gaussian(arg_keys[2], (KVH, KEYS, HD), 1.0, 6.0, ((0, 8), (1, 64))),
        "mask": draw_mask(jax.random.fold_in(arg_keys[5], 71), 0),
        "out_proj": gaussian(arg_keys[4], (QH * HD, D), (QH * HD) ** -0.5, 0.09375, ((0, 8), (1, 64))),
    }


def reference(queries, keys, values, mask, out_proj):
    shards = KEYS // CACHE_DEV
    query_heads = queries.astype(jnp.float32).reshape(QROWS, KVH, GROUP, HD)
    scale = 1.0 / jnp.sqrt(jnp.float32(HD))
    offset = jnp.log(jnp.float32(KEYS))

    def one_shard(total, index):
        start = (index * CACHE_DEV).astype(jnp.int32)
        key_part = lax.dynamic_slice_in_dim(keys, start, CACHE_DEV, 1).astype(jnp.float32)
        value_part = lax.dynamic_slice_in_dim(values, start, CACHE_DEV, 1).astype(jnp.float32)
        mask_part = lax.dynamic_slice_in_dim(mask, (index * (CACHE_DEV // BLK)).astype(jnp.int32), CACHE_DEV // BLK, 1)
        live = jnp.repeat(jnp.repeat(mask_part, BLK, axis=0), BLK, axis=1) > 0
        score = jnp.einsum('qhgd,hkd->hgqk', query_heads, key_part) * scale - offset
        weight = jnp.where(live[None, None], jax.nn.sigmoid(score), 0.0).astype(jnp.bfloat16)
        weight = lax.optimization_barrier(weight).astype(jnp.float32)
        return (total + jnp.einsum('hgqk,hkd->qhgd', weight, value_part), None)
    start_total = jnp.zeros((QROWS, KVH, GROUP, HD), jnp.float32)
    attended, unused = lax.scan(one_shard, start_total, jnp.arange(shards, dtype=jnp.int32))
    attended_bf = attended.reshape(QROWS, QH * HD).astype(jnp.bfloat16)
    return jnp.dot(attended_bf, out_proj, preferred_element_type=jnp.float32).astype(jnp.bfloat16)
```

```python
import functools
import math

import jax
import jax.numpy as jnp
from jax import lax
from jax.experimental import pallas as pl
from jax.experimental.pallas import tpu as pltpu
from jax.sharding import PartitionSpec as P

MESH = pl.DeviceIdType.MESH
BF = jnp.bfloat16
F32 = jnp.float32

NY, NZ = 4, 16
NH = 8
HD = 128
GROUP = 4
ROWS = 16
KEYS = 2048
BLK = 128
TILE = 256
UNITS = NZ // 2
SCALE = -math.log2(math.e) / math.sqrt(HD)
SHIFT = 2.0**-17


def kernel(
    q_hbm, k_hbm, v_hbm, mask_ref, w_hbm, o_ref,
    k_raw, k2t, v_buf, cm, q_buf, q2, p_send, y_recv, z_send, z_recv,
    a_send, a_recv, w_raw, w_buf, o_send, o_recv,
    loc, qr_s, qr_r, ql_s, ql_r, qy_s, qy_r, ps_s, ps_r, z_s, z_r,
    a_s, a_r, wr_s, wr_r, wl_s, wl_r, o_s, o_r,
):
    seq = lax.axis_index("seq")
    head = lax.axis_index("head")
    y, z = seq // NZ, lax.rem(seq, NZ)

    def zmod(value):
        return lax.rem(value + 2 * NZ, NZ)

    def ypeer(d):
        return lax.rem(y + d, NY)

    def at(yy, zz):
        return yy * NZ + zz

    def remote(src, dst, send, recv, to_seq, to_head):
        return pltpu.make_async_remote_copy(
            src_ref=src, dst_ref=dst, send_sem=send, recv_sem=recv,
            device_id=(to_seq, to_head), device_id_type=MESH,
        )

    right, left = at(y, zmod(z + 1)), at(y, zmod(z - 1))
    out_y = head // 2
    own_out = out_y == y

    q_load = pltpu.make_async_copy(q_hbm, q_buf.at[z, y], loc.at[0])
    k_load = pltpu.make_async_copy(k_hbm.at[0], k_raw, loc.at[1])
    v_load = pltpu.make_async_copy(v_hbm.at[0], v_buf, loc.at[2])
    w_load = pltpu.make_async_copy(w_hbm, w_raw, loc.at[3])
    q_load.start()
    k_load.start()
    w_load.start()
    v_load.start()

    barrier = pltpu.get_barrier_semaphore()

    def greet(to_seq, to_head):
        pl.semaphore_signal(barrier, inc=1, device_id=(to_seq, to_head), device_id_type=MESH)

    for d in range(1, NY):
        greet(at(ypeer(d), z), head)

    def greet_z(d, carry):
        greet(at(y, zmod(z + d)), head)
        return carry

    lax.fori_loop(1, NZ, greet_z, 0)
    for h in range(NH):
        @pl.when(jnp.logical_not(jnp.logical_and(own_out, head == h)))
        def _():
            greet(at(out_y, z), h)

    live = mask_ref[...] > 0
    cut = jnp.where(live, F32(SHIFT), F32(jnp.inf))
    for b in range(KEYS // BLK):
        wide = jnp.broadcast_to(cut[:, b : b + 1], (8, BLK))
        for r in range(8):
            cm[r, :, b * BLK : (b + 1) * BLK] = jnp.broadcast_to(wide[r : r + 1], (8, BLK))
    q_load.wait()
    pl.semaphore_wait(barrier, NY - 1 + NZ - 1 + NH - own_out.astype(jnp.int32))

    def q_ring_r(i, step):
        ref = q_buf.at[zmod(z - i), y]
        return remote(ref, ref, qr_s.at[i], qr_r.at[step], right, head)

    def q_ring_l(i, step):
        ref = q_buf.at[zmod(z + i), y]
        return remote(ref, ref, ql_s.at[i], ql_r.at[step], left, head)

    def q_hand(b):
        ref = q_buf.at[b, y]
        for d in range(1, NY):
            remote(ref, ref, qy_s.at[b], qy_r.at[b], at(ypeer(d), z), head).start()

    def three(b, send, recv):
        ref = y_recv.at[b]
        return remote(ref, ref, send, recv, right, head)

    q_ring_r(0, 0 + 1).start()
    q_ring_l(0, 0 + 1).start()
    q_hand(z)

    k_load.wait()
    keys_t = k_raw[...].T
    k2t[:HD, :] = keys_t
    k2t[HD:, :] = keys_t
    w_load.wait()
    half = w_raw.shape[0] // 2
    w_buf[z] = jnp.concatenate([w_raw[:half, :], w_raw[half:, :]], axis=1)
    v_load.wait()

    def w_ring_r(i, step):
        ref = w_buf.at[zmod(z - i)]
        return remote(ref, ref, wr_s.at[i], wr_r.at[step], right, head)

    def w_ring_l(i, step):
        ref = w_buf.at[zmod(z + i)]
        return remote(ref, ref, wl_s.at[i], wl_r.at[step], left, head)

    w_ring_r(0, 0 + 1).start()
    w_ring_l(0, 0 + 1).start()

    def attend(blocks):
        for n, b in enumerate(blocks):
            for yy in range(NY):
                for g in range(GROUP):
                    part = q_buf[b, yy, :, g * HD : (g + 1) * HD].astype(F32) * SCALE
                    high = part.astype(BF)
                    row = ((n * NY + yy) * GROUP + g) * ROWS
                    q2[row : row + ROWS, :HD] = high
                    q2[row : row + ROWS, HD:] = (part - high.astype(F32)).astype(BF)
        total = jnp.zeros((q2.shape[0], HD), F32)
        span = GROUP * ROWS
        for t in range(KEYS // TILE):
            cols = slice(t * TILE, (t + 1) * TILE)
            score = jnp.dot(q2[...], k2t[:, cols], preferred_element_type=F32)
            power = jnp.exp2(score)
            parts = []
            for n, b in enumerate(blocks):
                for yy in range(NY):
                    row = (n * NY + yy) * span
                    add = cm[yy * 2 + b // 8, :, cols]
                    group = power[row : row + span].reshape(span // 8, 8, TILE) + add[None]
                    parts.append(
                        pltpu.reciprocal(group, approx=True).reshape(span, TILE).astype(BF)
                    )
            weight = jnp.concatenate(parts, axis=0)
            total = total + jnp.dot(weight, v_buf[cols, :], preferred_element_type=F32)
        for n, b in enumerate(blocks):
            for yy in range(NY):
                for g in range(GROUP):
                    row = ((n * NY + yy) * GROUP + g) * ROWS
                    p_send[b, yy, :, g * HD : (g + 1) * HD] = (total[row : row + ROWS] * SHIFT).astype(BF)

    def hand_out(b):
        for d in range(1, NY):
            to = ypeer(d)
            remote(p_send.at[b, to], y_recv.at[b, d - 1], ps_s.at[b], ps_r.at[b], at(to, z), head).start()

    def z_copy(b):
        rel = zmod(b - z)
        return remote(z_send.at[b], z_recv.at[rel - 1], z_s.at[b], z_r, at(y, b), head)

    def gather_up(b, own):
        three(b, ps_s.at[b], ps_r.at[b]).wait_recv()
        total = p_send[b, y].astype(F32)
        for d in range(NY - 1):
            total = total + y_recv[b, d].astype(F32)
        z_send[b] = total.astype(BF)

        @pl.when(jnp.logical_not(own))
        def _():
            z_copy(b).start()

    def unit(u, carry):
        i = u + 1
        q_ring_r_in = zmod(z - i)
        q_ring_r(i, i).wait_recv()

        @pl.when(i < UNITS)
        def _():
            q_ring_r(i, i + 1).start()

        q_hand(q_ring_r_in)

        @pl.when(i < UNITS)
        def _():
            q_ring_l(i, i).wait_recv()

            @pl.when(i < UNITS - 1)
            def _():
                q_ring_l(i, i + 1).start()

            q_hand(zmod(z + i))

        @pl.when(u > 0)
        def _():
            w_ring_r(u, u).wait_recv()
            w_ring_r(u, u + 1).start()
            w_ring_l(u, u).wait_recv()

            @pl.when(u < UNITS - 1)
            def _():
                w_ring_l(u, u + 1).start()

        b0, b1 = zmod(z - i), zmod(z + u)
        three(b0, qy_s.at[b0], qy_r.at[b0]).wait_recv()
        three(b1, qy_s.at[b1], qy_r.at[b1]).wait_recv()
        attend((b0, b1))
        hand_out(b0)
        hand_out(b1)

        @pl.when(u > 0)
        def _():
            gather_up(zmod(z - u), False)
            gather_up(zmod(z + u - 1), u == 1)

        return carry

    lax.fori_loop(0, UNITS, unit, 0)
    gather_up(zmod(z - UNITS), False)
    gather_up(zmod(z + UNITS - 1), False)

    w_ring_r(UNITS, UNITS).wait_recv()

    remote(z_recv, z_recv, z_s.at[0], z_r, right, head).wait_recv()
    total = z_send[z].astype(F32)
    for n in range(NZ - 1):
        total = total + z_recv[n].astype(F32)
    a_send[...] = total.astype(BF)
    for d in range(1, NY):
        remote(a_send, a_recv.at[d - 1], a_s.at[d], a_r, at(ypeer(d), z), head).start()

    def left_all(b, carry):
        three(b, qy_s.at[b], qy_r.at[b]).wait_send()
        three(b, ps_s.at[b], ps_r.at[b]).wait_send()

        @pl.when(b != z)
        def _():
            z_copy(b).wait_send()

        return carry

    lax.fori_loop(0, NZ, left_all, 0)

    def left_ring(i, carry):
        q_ring_r(i, i).wait_send()
        w_ring_r(i, i).wait_send()

        @pl.when(i < UNITS - 1)
        def _():
            q_ring_l(i, i).wait_send()
            w_ring_l(i, i).wait_send()

        return carry

    lax.fori_loop(0, UNITS, left_ring, 0)

    remote(a_recv, a_recv, a_s.at[0], a_r, right, head).wait_recv()

    rows = [a_send[...]] + [a_recv[d] for d in range(NY - 1)]
    attended = jnp.concatenate(rows, axis=0)
    depth = attended.shape[1] // 2
    stacked = jnp.concatenate([attended[:, :depth], attended[:, depth:]], axis=0)
    count = NY * ROWS
    for c in range(2):
        for n in range(0, NZ // 2, 2):
            pair = []
            for m in range(2):
                full = jnp.dot(stacked, w_buf[c * (NZ // 2) + n + m], preferred_element_type=F32)
                pair.append(full[:count, :64] + full[count:, 64:])
            both = jnp.concatenate(pair, axis=1).astype(BF)
            for d in range(NY):
                o_send[d, c, :, n * 64 : (n + 2) * 64] = both[d * ROWS : (d + 1) * ROWS]

    def o_copy(d, c):
        to = lax.rem(y - d + NY, NY)
        return remote(o_send.at[d, c], o_recv.at[head], o_s.at[d, c], o_r, at(to, z), 2 * y + c)

    for d in range(NY):
        for c in range(2):
            if d == 0:
                mine = head == 2 * y + c

                @pl.when(mine)
                def _():
                    pltpu.make_async_copy(o_send.at[d, c], o_recv.at[head], o_r).start()

                @pl.when(jnp.logical_not(mine))
                def _():
                    o_copy(d, c).start()
            else:
                o_copy(d, c).start()

    for d in range(1, NY):
        remote(a_send, a_recv.at[d - 1], a_s.at[d], a_r, right, head).wait_send()
    remote(o_recv, o_recv, o_s.at[0, 0], o_r, right, head).wait_recv()
    total = o_recv[0].astype(F32)
    for n in range(1, NH):
        total = total + o_recv[n].astype(F32)
    o_ref[...] = total.astype(BF)
    for d in range(NY):
        for c in range(2):
            if d == 0:
                @pl.when(head != 2 * y + c)
                def _():
                    o_copy(d, c).wait_send()
            else:
                o_copy(d, c).wait_send()


def on_device(queries, keys, values, mask, out_proj):
    width = queries.shape[1]
    block = (ROWS, width)
    dma = pltpu.SemaphoreType.DMA
    return pl.pallas_call(
        kernel,
        out_shape=jax.ShapeDtypeStruct(block, BF),
        in_specs=[
            pl.BlockSpec(memory_space=pl.ANY),
            pl.BlockSpec(memory_space=pl.ANY),
            pl.BlockSpec(memory_space=pl.ANY),
            pl.BlockSpec(memory_space=pltpu.VMEM),
            pl.BlockSpec(memory_space=pl.ANY),
        ],
        out_specs=pl.BlockSpec(memory_space=pltpu.VMEM),
        scratch_shapes=[
            pltpu.VMEM((KEYS, HD), BF),
            pltpu.VMEM((2 * HD, KEYS), BF),
            pltpu.VMEM((KEYS, HD), BF),
            pltpu.VMEM((8, 8, KEYS), F32),
            pltpu.VMEM((NZ, NY) + block, BF),
            pltpu.VMEM((2 * NY * GROUP * ROWS, 2 * HD), BF),
            pltpu.VMEM((NZ, NY) + block, BF),
            pltpu.VMEM((NZ, NY - 1) + block, BF),
            pltpu.VMEM((NZ,) + block, BF),
            pltpu.VMEM((NZ - 1,) + block, BF),
            pltpu.VMEM(block, BF),
            pltpu.VMEM((NY - 1,) + block, BF),
            pltpu.VMEM(out_proj.shape, BF),
            pltpu.VMEM((NZ, out_proj.shape[0] // 2, 2 * out_proj.shape[1]), BF),
            pltpu.VMEM((NY, 2) + block, BF),
            pltpu.VMEM((NH,) + block, BF),
            dma((4,)),
            dma((UNITS + 1,)), dma((UNITS + 1,)), dma((UNITS + 1,)), dma((UNITS + 1,)),
            dma((NZ,)), dma((NZ,)),
            dma((NZ,)), dma((NZ,)),
            dma((NZ,)), dma,
            dma((NY,)), dma,
            dma((UNITS + 1,)), dma((UNITS + 1,)), dma((UNITS + 1,)), dma((UNITS + 1,)),
            dma((NY, 2)), dma,
        ],
        compiler_params=pltpu.CompilerParams(
            collective_id=0, has_side_effects=True, vmem_limit_bytes=40 * 1024 * 1024
        ),
        name="attend",
    )(queries, keys, values, mask, out_proj)


def solution(mesh):
    placed = (
        P("seq", "head"),
        P("head", "seq", None),
        P("head", "seq", None),
        P(None, "seq"),
        P("head", "seq"),
    )
    return jax.shard_map(
        on_device, mesh=mesh, in_specs=placed, out_specs=P("seq", "head"), check_vma=False
    )
```

```python
import functools
import math

import jax
import jax.numpy as jnp
from jax import lax
from jax.experimental import pallas as pl
from jax.experimental.pallas import tpu as pltpu
from jax.sharding import PartitionSpec as P

MESH = pl.DeviceIdType.MESH
BF = jnp.bfloat16
F32 = jnp.float32

NY, NZ = 4, 16
NH = 8
HD = 128
GROUP = 4
ROWS = 16
KEYS = 2048
BLK = 128
TILE = 256
UNITS = NZ // 2
SCALE = -math.log2(math.e) / math.sqrt(HD)
SHIFT = 2.0**-17


FIRST = (0, 3, 8, -6, 4, 5, 7, -1)
SECOND = (1, -3, 6, 2, -4, -5, -7, -2)
LAG = 3


def kernel(
    q_hbm, k_hbm, v_hbm, mask_ref, w_hbm, o_ref,
    k2, v_buf, cm, q_buf, q2, p_send, y_recv, z_send, z_recv,
    a_send, a_recv, w_buf, o_send, o_recv,
    loc, qz_s, qz_r, qf_s, qy_s, qy_r, ps_s, ps_r, z_s, z_r,
    a_s, a_r, w_s, wr_r, wl_r, o_s, o_r,
):
    seq = lax.axis_index("seq")
    head = lax.axis_index("head")
    y, z = seq // NZ, lax.rem(seq, NZ)

    def zmod(value):
        return lax.rem(value + 2 * NZ, NZ)

    def ypeer(d):
        return lax.rem(y + d, NY)

    def at(yy, zz):
        return yy * NZ + zz

    def remote(src, dst, send, recv, to_seq, to_head):
        return pltpu.make_async_remote_copy(
            src_ref=src, dst_ref=dst, send_sem=send, recv_sem=recv,
            device_id=(to_seq, to_head), device_id_type=MESH,
        )

    right, left = at(y, zmod(z + 1)), at(y, zmod(z - 1))
    out_y = head // 2
    own_out = out_y == y

    def arrived(ref, sem):
        remote(ref, ref, o_s, sem, right, head).wait_recv()

    def left_here(ref, sem):
        remote(ref, ref, sem, o_r, right, head).wait_send()

    k_load = pltpu.make_async_copy(k_hbm.at[0], k2.at[:, :HD], loc.at[1])
    k_again = pltpu.make_async_copy(k_hbm.at[0], k2.at[:, HD:], loc.at[2])
    q_load = pltpu.make_async_copy(q_hbm, q_buf.at[z, y], loc.at[0])
    v_load = pltpu.make_async_copy(v_hbm.at[0], v_buf, loc.at[3])
    w_load = pltpu.make_async_copy(w_hbm, w_buf.at[z], loc.at[4])
    q_load.start()
    w_load.start()
    k_load.start()
    k_again.start()
    v_load.start()

    barrier = pltpu.get_barrier_semaphore()

    def greet(to_seq, to_head):
        pl.semaphore_signal(barrier, inc=1, device_id=(to_seq, to_head), device_id_type=MESH)

    for d in range(1, NY):
        greet(at(ypeer(d), z), head)

    def greet_z(d, carry):
        greet(at(y, zmod(z + d)), head)
        return carry

    lax.fori_loop(1, NZ, greet_z, 0)
    for h in range(NH):
        @pl.when(jnp.logical_not(jnp.logical_and(own_out, head == h)))
        def _():
            greet(at(out_y, z), h)

    live = mask_ref[...] > 0
    cut = jnp.where(live, F32(SHIFT), F32(jnp.inf))
    for b in range(KEYS // BLK):
        wide = jnp.broadcast_to(cut[:, b : b + 1], (8, BLK))
        for r in range(8):
            cm[r, :, b * BLK : (b + 1) * BLK] = jnp.broadcast_to(wide[r : r + 1], (8, BLK))
    q_load.wait()
    pl.semaphore_wait(barrier, NY - 1 + NZ - 1 + NH - own_out.astype(jnp.int32))

    def q_copy(b, send, d):
        ref = q_buf.at[b, y]
        return remote(ref, ref, send, qz_r.at[b], at(y, zmod(z + d)), head)

    def q_hand(b):
        ref = q_buf.at[b, y]
        for d in range(1, NY):
            remote(ref, ref, qy_s, qy_r.at[b], at(ypeer(d), z), head).start()

    def q_take(offset, relay):
        b = zmod(z + offset)
        arrived(q_buf.at[b, y], qz_r.at[b])
        if relay:
            q_copy(b, qf_s, 1).start()
            q_copy(b, qf_s, -1).start()
        q_hand(b)

    for d in (1, -1, 3, -3):
        q_copy(z, qz_s, d).start()
    q_hand(z)
    for d in (6, -6, 8):
        q_copy(z, qz_s, d).start()

    def w_ring_r(i):
        ref = w_buf.at[zmod(z - i)]
        remote(ref, ref, w_s, wr_r.at[i + 1], right, head).start()

    def w_ring_l(i):
        ref = w_buf.at[zmod(z + i)]
        remote(ref, ref, w_s, wl_r.at[i + 1], left, head).start()

    def w_relay(i):
        arrived(w_buf.at[zmod(z - i)], wr_r.at[i])
        if i < UNITS:
            w_ring_r(i)
            arrived(w_buf.at[zmod(z + i)], wl_r.at[i])
        if i < UNITS - 1:
            w_ring_l(i)

    w_load.wait()
    w_ring_r(0)
    w_ring_l(0)

    k_load.wait()
    k_again.wait()
    v_load.wait()
    q_take(1, False)
    q_take(-1, False)
    q_take(3, True)
    q_take(-3, True)
    w_relay(1)

    def attend(blocks):
        for n, b in enumerate(blocks):
            for yy in range(NY):
                for g in range(GROUP):
                    part = q_buf[b, yy, :, g * HD : (g + 1) * HD].astype(F32) * SCALE
                    high = part.astype(BF)
                    row = ((n * NY + yy) * GROUP + g) * ROWS
                    q2[row : row + ROWS, :HD] = high
                    q2[row : row + ROWS, HD:] = (part - high.astype(F32)).astype(BF)
        total = jnp.zeros((q2.shape[0], HD), F32)
        span = GROUP * ROWS
        for t in range(KEYS // TILE):
            cols = slice(t * TILE, (t + 1) * TILE)
            score = lax.dot_general(q2[...], k2[cols, :], (((1,), (1,)), ((), ())), preferred_element_type=F32)
            power = jnp.exp2(score)
            parts = []
            for n, b in enumerate(blocks):
                for yy in range(NY):
                    row = (n * NY + yy) * span
                    add = cm[yy * 2 + b // 8, :, cols]
                    group = power[row : row + span].reshape(span // 8, 8, TILE) + add[None]
                    parts.append(
                        pltpu.reciprocal(group, approx=True).reshape(span, TILE).astype(BF)
                    )
            weight = jnp.concatenate(parts, axis=0)
            total = total + jnp.dot(weight, v_buf[cols, :], preferred_element_type=F32)
        for n, b in enumerate(blocks):
            for yy in range(NY):
                for g in range(GROUP):
                    row = ((n * NY + yy) * GROUP + g) * ROWS
                    p_send[b, yy, :, g * HD : (g + 1) * HD] = (total[row : row + ROWS] * SHIFT).astype(BF)

    def hand_out(b):
        for d in range(1, NY):
            to = ypeer(d)
            remote(p_send.at[b, to], y_recv.at[b, d - 1], ps_s, ps_r.at[b], at(to, z), head).start()

    def gather_up(b, own):
        arrived(y_recv.at[b], ps_r.at[b])
        total = p_send[b, y].astype(F32)
        for d in range(NY - 1):
            total = total + y_recv[b, d].astype(F32)
        z_send[b] = total.astype(BF)

        @pl.when(jnp.logical_not(own))
        def _():
            rel = zmod(b - z)
            remote(z_send.at[b], z_recv.at[rel - 1], z_s, z_r, at(y, b), head).start()

    def pick(u, table):
        value = jnp.int32(table[0])
        for n in range(1, UNITS):
            value = jnp.where(u == n, table[n], value)
        return zmod(z + value)

    def gather_unit(u):
        gather_up(pick(u, FIRST), u == 0)
        gather_up(pick(u, SECOND), False)

    def unit(u, carry):
        b0, b1 = pick(u, FIRST), pick(u, SECOND)
        arrived(y_recv.at[b0], qy_r.at[b0])
        arrived(y_recv.at[b1], qy_r.at[b1])
        attend((b0, b1))
        hand_out(b0)
        hand_out(b1)

        @pl.when(u == 0)
        def _():
            q_take(8, False)
            q_take(6, True)
            q_take(-6, True)
            for d in (2, -2, 4, -4):
                q_take(d, False)

        @pl.when(u == 1)
        def _():
            w_relay(2)

        @pl.when(u == 2)
        def _():
            for d in (5, -5, 7, -7):
                q_take(d, False)

        @pl.when(u == 3)
        def _():
            w_relay(3)

        @pl.when(u == 5)
        def _():
            w_relay(4)

        @pl.when(u >= LAG)
        def _():
            gather_unit(u - LAG)

        return carry

    lax.fori_loop(0, UNITS, unit, 0)
    w_relay(5)

    def collect(u, carry):
        gather_unit(u)
        return carry

    lax.fori_loop(UNITS - LAG, UNITS, collect, 0)
    w_relay(6)

    arrived(z_recv, z_r)
    total = z_send[z].astype(F32)
    for n in range(NZ - 1):
        total = total + z_recv[n].astype(F32)
    a_send[...] = total.astype(BF)
    for d in range(1, NY):
        remote(a_send, a_recv.at[d - 1], a_s, a_r, at(ypeer(d), z), head).start()
    w_relay(7)

    left_here(z_recv.at[: 7], qz_s)
    left_here(z_recv.at[: 8], qf_s)
    left_here(y_recv, qy_s)
    left_here(y_recv, ps_s)
    left_here(z_recv, z_s)
    arrived(a_recv, a_r)
    w_relay(8)

    rows = [a_send[...]] + [a_recv[d] for d in range(NY - 1)]
    attended = jnp.concatenate(rows, axis=0)
    wide = NZ // 2
    for c in range(2):
        columns = w_buf[c * wide : (c + 1) * wide].reshape(wide * w_buf.shape[1], w_buf.shape[2])
        share = lax.dot_general(attended, columns, (((1,), (1,)), ((), ())), preferred_element_type=F32)
        share = share.astype(BF)
        for d in range(NY):
            o_send[d, c] = share[d * ROWS : (d + 1) * ROWS]
            to = lax.rem(y - d + NY, NY)
            copy = remote(o_send.at[d, c], o_recv.at[head], o_s, o_r, at(to, z), 2 * y + c)
            if d == 0:
                mine = head == 2 * y + c

                @pl.when(mine)
                def _():
                    pltpu.make_async_copy(o_send.at[d, c], o_recv.at[head], o_r).start()

                @pl.when(jnp.logical_not(mine))
                def _():
                    copy.start()
            else:
                copy.start()

    left_here(a_recv, a_s)
    left_here(w_buf.at[: NZ - 1], w_s)
    arrived(o_recv, o_r)
    total = o_recv[0].astype(F32)
    for n in range(1, NH):
        total = total + o_recv[n].astype(F32)
    o_ref[...] = total.astype(BF)

    @pl.when(own_out)
    def _():
        left_here(o_recv.at[: NH - 1], o_s)

    @pl.when(jnp.logical_not(own_out))
    def _():
        left_here(o_recv, o_s)


def on_device(queries, keys, values, mask, out_proj):
    width = queries.shape[1]
    block = (ROWS, width)
    dma = pltpu.SemaphoreType.DMA
    return pl.pallas_call(
        kernel,
        out_shape=jax.ShapeDtypeStruct(block, BF),
        in_specs=[
            pl.BlockSpec(memory_space=pl.ANY),
            pl.BlockSpec(memory_space=pl.ANY),
            pl.BlockSpec(memory_space=pl.ANY),
            pl.BlockSpec(memory_space=pltpu.VMEM),
            pl.BlockSpec(memory_space=pl.ANY),
        ],
        out_specs=pl.BlockSpec(memory_space=pltpu.VMEM),
        scratch_shapes=[
            pltpu.VMEM((KEYS, 2 * HD), BF),
            pltpu.VMEM((KEYS, HD), BF),
            pltpu.VMEM((8, 8, KEYS), F32),
            pltpu.VMEM((NZ, NY) + block, BF),
            pltpu.VMEM((2 * NY * GROUP * ROWS, 2 * HD), BF),
            pltpu.VMEM((NZ, NY) + block, BF),
            pltpu.VMEM((NZ, NY - 1) + block, BF),
            pltpu.VMEM((NZ,) + block, BF),
            pltpu.VMEM((NZ - 1,) + block, BF),
            pltpu.VMEM(block, BF),
            pltpu.VMEM((NY - 1,) + block, BF),
            pltpu.VMEM((NZ,) + out_proj.shape[::-1], BF),
            pltpu.VMEM((NY, 2) + block, BF),
            pltpu.VMEM((NH,) + block, BF),
            dma((5,)),
            dma, dma((NZ,)), dma,
            dma, dma((NZ,)),
            dma, dma((NZ,)),
            dma, dma,
            dma, dma,
            dma, dma((UNITS + 1,)), dma((UNITS + 1,)),
            dma, dma,
        ],
        compiler_params=pltpu.CompilerParams(
            collective_id=0, has_side_effects=True, vmem_limit_bytes=60 * 1024 * 1024
        ),
        name="attend",
    )(queries, keys, values, mask, out_proj.T)


def solution(mesh):
    placed = (
        P("seq", "head"),
        P("head", "seq", None),
        P("head", "seq", None),
        P(None, "seq"),
        P("head", "seq"),
    )
    return jax.shard_map(
        on_device, mesh=mesh, in_specs=placed, out_specs=P("seq", "head"), check_vma=False
    )
```

```python
import functools
import math

import jax
import jax.numpy as jnp
from jax import lax
from jax.experimental import pallas as pl
from jax.experimental.pallas import tpu as pltpu
from jax.sharding import PartitionSpec as P

MESH = pl.DeviceIdType.MESH
BF = jnp.bfloat16
F32 = jnp.float32

NY, NZ = 4, 16
NX = 4
HD = 128
GROUP = 4
ROWS = 16
KEYS = 2048
BLK = 128
TILE = 256
UNITS = NZ // 2
SCALE = -math.log2(math.e) / math.sqrt(HD)
SHIFT = 2.0**-17


FIRST = (0, 5, 8, 7, 6, 4, 3, -1)
SECOND = (1, -5, -2, -7, -6, -4, -3, 2)
LAST = (FIRST[-1], SECOND[-1])
FAR = (6, 7)
SLOTS = (1, -2, 3, -3, 8, 4, -4, 5, -5)
NEAR = (1, -1, 2, -2, 3, -3, 4, -4, 5, -5, 8)
LAG = 2


def kernel(
    q_hbm, k_hbm, v_hbm, mask_hbm, w_hbm, o_ref,
    m_buf, k2, v_buf, cm, q_buf, q2, p_send, y_recv, z_send, z_recv, n_recv, d_recv,
    a_send, a_recv, w_buf, c_send, c_recv, o_send, o_recv,
    loc, qz_s, qz_r, qf_s, qb_s, qb_r, qy_s, qy_r, ps_s, ps_r, z_s, z_r, n_s, n_r, d_s, d_r,
    a_s, a_r, w_s, wr_r, wl_r, c_s, c_r, o_s, o_r,
):
    seq = lax.axis_index("seq")
    head = lax.axis_index("head")
    y, z = seq // NZ, lax.rem(seq, NZ)

    def zmod(value):
        return lax.rem(value + 2 * NZ, NZ)

    def ypeer(d):
        return lax.rem(y + d, NY)

    def at(yy, zz):
        return yy * NZ + zz

    def remote(src, dst, send, recv, to_seq, to_head):
        return pltpu.make_async_remote_copy(
            src_ref=src, dst_ref=dst, send_sem=send, recv_sem=recv,
            device_id=(to_seq, to_head), device_id_type=MESH,
        )

    right, left = at(y, zmod(z + 1)), at(y, zmod(z - 1))
    x, core = head // 2, lax.rem(head, 2)
    partner = head + 1 - 2 * core
    out_y = x
    own_out = out_y == y

    def arrived(ref, sem):
        remote(ref, ref, o_s, sem, right, head).wait_recv()

    def left_here(ref, sem):
        remote(ref, ref, sem, o_r, right, head).wait_send()

    k_load = pltpu.make_async_copy(k_hbm.at[0], k2.at[:, :HD], loc.at[1])
    k_again = pltpu.make_async_copy(k_hbm.at[0], k2.at[:, HD:], loc.at[2])
    q_load = pltpu.make_async_copy(q_hbm, q_buf.at[z, y], loc.at[0])
    v_load = pltpu.make_async_copy(v_hbm.at[0], v_buf, loc.at[3])
    m_load = pltpu.make_async_copy(mask_hbm, m_buf, loc.at[5])
    w_load = pltpu.make_async_copy(w_hbm, w_buf.at[z], loc.at[4])
    q_load.start()
    m_load.start()
    w_load.start()
    k_load.start()
    k_again.start()
    v_load.start()

    barrier = pltpu.get_barrier_semaphore()

    def greet(to_seq, to_head):
        pl.semaphore_signal(barrier, inc=1, device_id=(to_seq, to_head), device_id_type=MESH)

    for d in range(1, NY):
        greet(at(ypeer(d), z), head)

    for d in NEAR:
        greet(at(y, zmod(z + d)), head)
    for d in range(1, NY):
        for offset in LAST:
            greet(at(ypeer(d), zmod(z - offset)), head)
    greet(seq, partner)
    for n in range(NX):
        @pl.when(jnp.logical_not(jnp.logical_and(own_out, x == n)))
        def _():
            greet(at(out_y, z), 2 * n + core)

    m_load.wait()
    live = m_buf[...] > 0
    cut = jnp.where(live, F32(SHIFT), F32(jnp.inf))
    for b in range(KEYS // BLK):
        wide = jnp.broadcast_to(cut[:, b : b + 1], (8, BLK))
        for r in range(8):
            cm[r, :, b * BLK : (b + 1) * BLK] = jnp.broadcast_to(wide[r : r + 1], (8, BLK))
    q_load.wait()
    pl.semaphore_wait(barrier, NY - 1 + len(NEAR) + len(LAST) * (NY - 1) + 1 + NX - own_out.astype(jnp.int32))

    def q_copy(b, send, d):
        ref = q_buf.at[b, y]
        return remote(ref, ref, send, qz_r.at[b], at(y, zmod(z + d)), head)

    def q_hand(b):
        ref = q_buf.at[b, y]
        for d in range(1, NY):
            remote(ref, ref, qy_s, qy_r.at[b], at(ypeer(d), z), head).start()

    def q_take(offset):
        b = zmod(z + offset)
        arrived(q_buf.at[b, y], qz_r.at[b])
        if offset in (5, -5):
            for d in (2, 1, -1):
                q_copy(b, qf_s, d if offset < 0 else -d).start()
        q_hand(b)

    def q_pass(b, to):
        ref = q_buf.at[b]
        remote(ref, ref, qb_s, qb_r.at[b], to, head).start()

    def q_ring(i):
        for b, to in ((zmod(z - i), right), (zmod(z + i), left)):
            arrived(q_buf.at[b], qb_r.at[b])
            if i < 3:
                q_pass(b, to)

    for d in (5, -5):
        q_copy(z, qz_s, d).start()
    q_hand(z)
    q_copy(z, qz_s, 8).start()

    def w_ring_r(i):
        ref = w_buf.at[zmod(z - i)]
        remote(ref, ref, w_s, wr_r.at[i + 1], right, head).start()

    def w_ring_l(i):
        ref = w_buf.at[zmod(z + i)]
        remote(ref, ref, w_s, wl_r.at[i + 1], left, head).start()

    def w_relay(i):
        arrived(w_buf.at[zmod(z - i)], wr_r.at[i])
        if i < UNITS:
            w_ring_r(i)
            arrived(w_buf.at[zmod(z + i)], wl_r.at[i])
        if i < UNITS - 1:
            w_ring_l(i)

    w_load.wait()
    w_ring_r(0)
    w_ring_l(0)

    k_load.wait()
    k_again.wait()
    v_load.wait()
    arrived(y_recv.at[z], qy_r.at[z])
    q_pass(z, right)
    q_pass(z, left)
    w_relay(1)
    q_take(5)
    q_take(-5)
    q_ring(1)

    def attend(blocks):
        for n, b in enumerate(blocks):
            for yy in range(NY):
                for g in range(GROUP):
                    part = q_buf[b, yy, :, g * HD : (g + 1) * HD].astype(F32) * SCALE
                    high = part.astype(BF)
                    row = ((n * NY + yy) * GROUP + g) * ROWS
                    q2[row : row + ROWS, :HD] = high
                    q2[row : row + ROWS, HD:] = (part - high.astype(F32)).astype(BF)
        total = jnp.zeros((q2.shape[0], HD), F32)
        span = GROUP * ROWS
        for t in range(KEYS // TILE):
            cols = slice(t * TILE, (t + 1) * TILE)
            score = lax.dot_general(q2[...], k2[cols, :], (((1,), (1,)), ((), ())), preferred_element_type=F32)
            power = jnp.exp2(score)
            parts = []
            for n, b in enumerate(blocks):
                for yy in range(NY):
                    row = (n * NY + yy) * span
                    add = cm[yy * 2 + b // 8, :, cols]
                    group = power[row : row + span].reshape(span // 8, 8, TILE) + add[None]
                    parts.append(
                        pltpu.reciprocal(group, approx=True).reshape(span, TILE).astype(BF)
                    )
            weight = jnp.concatenate(parts, axis=0)
            total = total + jnp.dot(weight, v_buf[cols, :], preferred_element_type=F32)
        for n, b in enumerate(blocks):
            for yy in range(NY):
                for g in range(GROUP):
                    row = ((n * NY + yy) * GROUP + g) * ROWS
                    p_send[b, yy, :, g * HD : (g + 1) * HD] = (total[row : row + ROWS] * SHIFT).astype(BF)

    def hand_out(b):
        for d in range(1, NY):
            to = ypeer(d)
            remote(p_send.at[b, to], y_recv.at[b, d - 1], ps_s, ps_r.at[b], at(to, z), head).start()

    def add_up(b, total):
        total = total + p_send[b, y].astype(F32)
        for d in range(NY - 1):
            total = total + y_recv[b, d].astype(F32)
        z_send[b] = total.astype(BF)

    def to_owner(b, offset):
        remote(z_send.at[b], z_recv.at[SLOTS.index(offset)], z_s, z_r, at(y, b), head).start()

    def gather_up(b, u, table):
        arrived(y_recv.at[b], ps_r.at[b])
        add_up(b, jnp.zeros(z_send.shape[1:], F32))
        for n, offset in enumerate(table):
            if offset in (0, 5, -5) or n == UNITS - 1:
                continue

            @pl.when(u == n)
            def _(offset=offset):
                if abs(offset) in FAR:
                    side = int(offset < 0)
                    node = at(y, zmod(b + (5 if side else -5)))
                    slot = n_recv.at[side, FAR.index(abs(offset))]
                    remote(z_send.at[b], slot, n_s, n_r.at[side], node, head).start()
                else:
                    to_owner(b, offset)

    def gather_far(side):
        b = zmod(z + (-5 if side else 5))
        arrived(y_recv.at[b], ps_r.at[b])
        arrived(n_recv.at[side], n_r.at[side])
        total = n_recv[side, 0].astype(F32)
        for n in range(1, len(FAR)):
            total = total + n_recv[side, n].astype(F32)
        add_up(b, total)
        to_owner(b, -5 if side else 5)

    def pick(u, table):
        value = jnp.int32(table[0])
        for n in range(1, UNITS):
            value = jnp.where(u == n, table[n], value)
        return zmod(z + value)

    def gather_unit(u):
        @pl.when(u != 1)
        def _():
            gather_up(pick(u, FIRST), u, FIRST)
            gather_up(pick(u, SECOND), u, SECOND)

    def unit(u, carry):
        b0, b1 = pick(u, FIRST), pick(u, SECOND)

        @pl.when(jnp.logical_and(u >= 1, u <= 5))
        def _():
            arrived(y_recv.at[b0], qy_r.at[b0])

            @pl.when(u != 2)
            def _():
                arrived(y_recv.at[b1], qy_r.at[b1])

        attend((b0, b1))

        @pl.when(u < UNITS - 1)
        def _():
            hand_out(b0)
            hand_out(b1)

        @pl.when(u == UNITS - 1)
        def _():
            for n, b in enumerate((b0, b1)):
                for d in range(NY):
                    to = ypeer(d)
                    remote(p_send.at[b, to], d_recv.at[n, d], d_s, d_r, at(to, b), head).start()

        @pl.when(u == 0)
        def _():
            for d in (8, 7, -7):
                q_take(d)
            w_relay(2)

        @pl.when(u == 1)
        def _():
            for d in (6, -6, 4, -4):
                q_take(d)
            q_ring(2)

        @pl.when(u == 2)
        def _():
            w_relay(3)

        @pl.when(u == 4)
        def _():
            w_relay(4)

        @pl.when(u == 5)
        def _():
            q_ring(3)

        @pl.when(u == 6)
        def _():
            w_relay(5)

        @pl.when(u >= LAG)
        def _():
            gather_unit(u - LAG)

        return carry

    lax.fori_loop(0, UNITS, unit, 0)
    w_relay(6)

    for side in range(2):
        gather_far(side)
    gather_unit(UNITS - 2)
    w_relay(7)

    arrived(z_recv, z_r)
    arrived(d_recv, d_r)
    total = z_send[z].astype(F32)
    for n in range(len(LAST)):
        for d in range(NY):
            total = total + d_recv[n, d].astype(F32)
    for n in range(len(SLOTS)):
        total = total + z_recv[n].astype(F32)
    a_send[...] = total.astype(BF)
    for d in range(1, NY):
        remote(a_send, a_recv.at[d - 1], a_s, a_r, at(ypeer(d), z), head).start()

    left_here(z_recv.at[:3], qz_s)
    left_here(z_recv.at[:6], qf_s)
    left_here(y_recv.at[:8], qb_s)
    left_here(y_recv.at[:10], qy_s)
    left_here(n_recv, n_s)
    left_here(y_recv.at[: NZ - len(LAST)], ps_s)
    left_here(d_recv, d_s)
    left_here(z_recv, z_s)
    arrived(a_recv, a_r)
    w_relay(8)

    rows = [a_send[...]] + [a_recv[d] for d in range(NY - 1)]
    attended = jnp.concatenate(rows, axis=0)
    wide = NZ // 2

    def project(c):
        columns = w_buf[pl.ds(c * wide, wide)].reshape(wide * w_buf.shape[1], w_buf.shape[2])
        return lax.dot_general(attended, columns, (((1,), (1,)), ((), ())), preferred_element_type=F32)

    c_send[...] = project(1 - core).astype(BF)
    swap = remote(c_send, c_recv, c_s, c_r, seq, partner)
    swap.start()
    share = project(core)
    swap.wait_recv()
    o_send[...] = (share + c_recv[...].astype(F32)).astype(BF).reshape(o_send.shape)
    for d in range(NY):
        to = lax.rem(y - d + NY, NY)
        copy = remote(o_send.at[d], o_recv.at[x], o_s, o_r, at(to, z), 2 * y + core)
        if d == 0:
            @pl.when(own_out)
            def _():
                pltpu.make_async_copy(o_send.at[0], o_recv.at[x], o_r).start()

            @pl.when(jnp.logical_not(own_out))
            def _():
                copy.start()
        else:
            copy.start()

    swap.wait_send()
    left_here(a_recv, a_s)
    left_here(w_buf.at[: NZ - 1], w_s)
    arrived(o_recv, o_r)
    total = o_recv[0].astype(F32)
    for n in range(1, NX):
        total = total + o_recv[n].astype(F32)
    o_ref[...] = total.astype(BF)

    @pl.when(own_out)
    def _():
        left_here(o_recv.at[: NX - 1], o_s)

    @pl.when(jnp.logical_not(own_out))
    def _():
        left_here(o_recv, o_s)


def on_device(queries, keys, values, mask, out_proj):
    width = queries.shape[1]
    block = (ROWS, width)
    dma = pltpu.SemaphoreType.DMA
    return pl.pallas_call(
        kernel,
        out_shape=jax.ShapeDtypeStruct(block, BF),
        in_specs=[pl.BlockSpec(memory_space=pltpu.HBM)] * 5,
        out_specs=pl.BlockSpec(memory_space=pltpu.VMEM),
        scratch_shapes=[
            pltpu.VMEM(mask.shape, mask.dtype),
            pltpu.VMEM((KEYS, 2 * HD), BF),
            pltpu.VMEM((KEYS, HD), BF),
            pltpu.VMEM((8, 8, KEYS), F32),
            pltpu.VMEM((NZ, NY) + block, BF),
            pltpu.VMEM((2 * NY * GROUP * ROWS, 2 * HD), BF),
            pltpu.VMEM((NZ, NY) + block, BF),
            pltpu.VMEM((NZ, NY - 1) + block, BF),
            pltpu.VMEM((NZ,) + block, BF),
            pltpu.VMEM((len(SLOTS),) + block, BF),
            pltpu.VMEM((2, len(FAR)) + block, BF),
            pltpu.VMEM((len(LAST), NY) + block, BF),
            pltpu.VMEM(block, BF),
            pltpu.VMEM((NY - 1,) + block, BF),
            pltpu.VMEM((NZ,) + out_proj.shape[::-1], BF),
            pltpu.VMEM((NY * ROWS, width), BF),
            pltpu.VMEM((NY * ROWS, width), BF),
            pltpu.VMEM((NY,) + block, BF),
            pltpu.VMEM((NX,) + block, BF),
            dma((6,)),
            dma, dma((NZ,)), dma, dma, dma((NZ,)),
            dma, dma((NZ,)),
            dma, dma((NZ,)),
            dma, dma, dma, dma((2,)), dma, dma,
            dma, dma,
            dma, dma((UNITS + 1,)), dma((UNITS + 1,)),
            dma, dma, dma, dma,
        ],
        compiler_params=pltpu.CompilerParams(
            collective_id=0, has_side_effects=True, vmem_limit_bytes=40 * 1024 * 1024
        ),
        name="attend",
    )(*(pltpu.with_memory_space_constraint(a, pltpu.HBM) for a in (queries, keys, values, mask, out_proj.T)))


def solution(mesh):
    placed = (
        P("seq", "head"),
        P("head", "seq", None),
        P("head", "seq", None),
        P(None, "seq"),
        P("head", "seq"),
    )
    return jax.shard_map(
        on_device, mesh=mesh, in_specs=placed, out_specs=P("seq", "head"), check_vma=False
    )
```

```python
import functools
import math

import jax
import jax.numpy as jnp
from jax import lax
from jax.experimental import pallas as pl
from jax.experimental.pallas import tpu as pltpu
from jax.sharding import PartitionSpec as P

MESH = pl.DeviceIdType.MESH
BF = jnp.bfloat16
F32 = jnp.float32

NY, NZ = 4, 16
NX = 4
HD = 128
GROUP = 4
ROWS = 16
KEYS = 2048
BLK = 128
TILE = 256
UNITS = NZ // 2
SCALE = -math.log2(math.e) / math.sqrt(HD)
SHIFT = 2.0**-17


FIRST = (0, 5, 8, 7, 6, 4, 3, -1)
SECOND = (1, -5, -2, -7, -6, -4, -3, 2)
LAST = (FIRST[-1], SECOND[-1])
FAR = (6, 7)
SLOTS = (1, -2, 3, -3, 8, 4, -4, 5, -5)
NEAR = (1, -1, 2, -2, 3, -3, 4, -4, 5, -5, 8)
LAG = 2


def kernel(
    q_hbm, k_hbm, v_hbm, mask_hbm, w_hbm, o_ref,
    m_buf, k2, v_buf, cm, q_buf, q2, p_send, y_recv, z_send, z_recv, n_recv, d_recv,
    a_send, a_recv, w_buf, w_other, o_send, o_recv,
    loc, qz_s, qz_r, qf_s, qb_s, qb_r, qy_s, qy_r, ps_s, ps_r, z_s, z_r, n_s, n_r, d_s, d_r,
    a_s, a_r, w_s, wr_r, wl_r, wc_s, wc_r, o_s, o_r,
):
    seq = lax.axis_index("seq")
    head = lax.axis_index("head")
    y, z = seq // NZ, lax.rem(seq, NZ)

    def zmod(value):
        return lax.rem(value + 2 * NZ, NZ)

    def ypeer(d):
        return lax.rem(y + d, NY)

    def at(yy, zz):
        return yy * NZ + zz

    def remote(src, dst, send, recv, to_seq, to_head):
        return pltpu.make_async_remote_copy(
            src_ref=src, dst_ref=dst, send_sem=send, recv_sem=recv,
            device_id=(to_seq, to_head), device_id_type=MESH,
        )

    right, left = at(y, zmod(z + 1)), at(y, zmod(z - 1))
    x, core = head // 2, lax.rem(head, 2)
    partner = head + 1 - 2 * core
    out_y = x
    own_out = out_y == y

    def arrived(ref, sem):
        remote(ref, ref, o_s, sem, right, head).wait_recv()

    def left_here(ref, sem):
        remote(ref, ref, sem, o_r, right, head).wait_send()

    k_load = pltpu.make_async_copy(k_hbm.at[0], k2.at[:, :HD], loc.at[1])
    k_again = pltpu.make_async_copy(k_hbm.at[0], k2.at[:, HD:], loc.at[2])
    q_load = pltpu.make_async_copy(q_hbm, q_buf.at[z, y], loc.at[0])
    v_load = pltpu.make_async_copy(v_hbm.at[0], v_buf, loc.at[3])
    m_load = pltpu.make_async_copy(mask_hbm, m_buf, loc.at[5])
    w_load = pltpu.make_async_copy(w_hbm, w_buf.at[z], loc.at[4])
    q_load.start()
    m_load.start()
    w_load.start()
    k_load.start()
    k_again.start()
    v_load.start()

    barrier = pltpu.get_barrier_semaphore()

    def greet(to_seq, to_head):
        pl.semaphore_signal(barrier, inc=1, device_id=(to_seq, to_head), device_id_type=MESH)

    for d in range(1, NY):
        greet(at(ypeer(d), z), head)

    for d in NEAR:
        greet(at(y, zmod(z + d)), head)
    for d in range(1, NY):
        for offset in LAST:
            greet(at(ypeer(d), zmod(z - offset)), head)
    for d in range(NY):
        greet(at(ypeer(d), z), partner)
    for n in range(NX):
        @pl.when(jnp.logical_not(jnp.logical_and(own_out, x == n)))
        def _():
            greet(at(out_y, z), 2 * n + core)

    m_load.wait()
    live = m_buf[...] > 0
    cut = jnp.where(live, F32(SHIFT), F32(jnp.inf))
    for b in range(KEYS // BLK):
        wide = jnp.broadcast_to(cut[:, b : b + 1], (8, BLK))
        for r in range(8):
            cm[r, :, b * BLK : (b + 1) * BLK] = jnp.broadcast_to(wide[r : r + 1], (8, BLK))
    q_load.wait()
    pl.semaphore_wait(barrier, NY - 1 + len(NEAR) + len(LAST) * (NY - 1) + NY + NX - own_out.astype(jnp.int32))

    def q_copy(b, send, d):
        ref = q_buf.at[b, y]
        return remote(ref, ref, send, qz_r.at[b], at(y, zmod(z + d)), head)

    def q_hand(b):
        ref = q_buf.at[b, y]
        for d in range(1, NY):
            remote(ref, ref, qy_s, qy_r.at[b], at(ypeer(d), z), head).start()

    def q_take(offset):
        b = zmod(z + offset)
        arrived(q_buf.at[b, y], qz_r.at[b])
        if offset in (5, -5):
            for d in (2, 1, -1):
                q_copy(b, qf_s, d if offset < 0 else -d).start()
        q_hand(b)

    def q_pass(b, to):
        ref = q_buf.at[b]
        remote(ref, ref, qb_s, qb_r.at[b], to, head).start()

    def q_ring(i):
        for b, to in ((zmod(z - i), right), (zmod(z + i), left)):
            arrived(q_buf.at[b], qb_r.at[b])
            if i < 3:
                q_pass(b, to)

    for d in (5, -5):
        q_copy(z, qz_s, d).start()
    q_hand(z)
    q_copy(z, qz_s, 8).start()

    def w_ring_r(i):
        ref = w_buf.at[zmod(z - i)]
        remote(ref, ref, w_s, wr_r.at[i + 1], right, head).start()

    def w_ring_l(i):
        ref = w_buf.at[zmod(z + i)]
        remote(ref, ref, w_s, wl_r.at[i + 1], left, head).start()

    wide = NZ // 2

    def w_share(b):
        @pl.when(b // wide != core)
        def _():
            remote(w_buf.at[b], w_other.at[lax.rem(b, wide)], wc_s, wc_r, seq, partner).start()

    def w_relay(i):
        arrived(w_buf.at[zmod(z - i)], wr_r.at[i])
        if i < UNITS:
            w_ring_r(i)
        w_share(zmod(z - i))
        if i < UNITS:
            arrived(w_buf.at[zmod(z + i)], wl_r.at[i])
            if i < UNITS - 1:
                w_ring_l(i)
            w_share(zmod(z + i))

    w_load.wait()
    w_ring_r(0)
    w_ring_l(0)
    w_share(z)

    k_load.wait()
    k_again.wait()
    v_load.wait()
    arrived(y_recv.at[z], qy_r.at[z])
    q_pass(z, right)
    q_pass(z, left)
    w_relay(1)
    q_take(5)
    q_take(-5)
    q_ring(1)

    def attend(blocks):
        for n, b in enumerate(blocks):
            for yy in range(NY):
                for g in range(GROUP):
                    part = q_buf[b, yy, :, g * HD : (g + 1) * HD].astype(F32) * SCALE
                    high = part.astype(BF)
                    row = ((n * NY + yy) * GROUP + g) * ROWS
                    q2[row : row + ROWS, :HD] = high
                    q2[row : row + ROWS, HD:] = (part - high.astype(F32)).astype(BF)
        total = jnp.zeros((q2.shape[0], HD), F32)
        span = GROUP * ROWS
        for t in range(KEYS // TILE):
            cols = slice(t * TILE, (t + 1) * TILE)
            score = lax.dot_general(q2[...], k2[cols, :], (((1,), (1,)), ((), ())), preferred_element_type=F32)
            power = jnp.exp2(score)
            parts = []
            for n, b in enumerate(blocks):
                for yy in range(NY):
                    row = (n * NY + yy) * span
                    add = cm[yy * 2 + b // 8, :, cols]
                    group = power[row : row + span].reshape(span // 8, 8, TILE) + add[None]
                    parts.append(
                        pltpu.reciprocal(group, approx=True).reshape(span, TILE).astype(BF)
                    )
            weight = jnp.concatenate(parts, axis=0)
            total = total + jnp.dot(weight, v_buf[cols, :], preferred_element_type=F32)
        for n, b in enumerate(blocks):
            for yy in range(NY):
                for g in range(GROUP):
                    row = ((n * NY + yy) * GROUP + g) * ROWS
                    p_send[b, yy, :, g * HD : (g + 1) * HD] = (total[row : row + ROWS] * SHIFT).astype(BF)

    def hand_out(b):
        for d in range(1, NY):
            to = ypeer(d)
            remote(p_send.at[b, to], y_recv.at[b, d - 1], ps_s, ps_r.at[b], at(to, z), head).start()

    def add_up(b, total):
        total = total + p_send[b, y].astype(F32)
        for d in range(NY - 1):
            total = total + y_recv[b, d].astype(F32)
        z_send[b] = total.astype(BF)

    def to_owner(b, offset):
        remote(z_send.at[b], z_recv.at[SLOTS.index(offset)], z_s, z_r, at(y, b), head).start()

    def gather_up(b, u, table):
        arrived(y_recv.at[b], ps_r.at[b])
        add_up(b, jnp.zeros(z_send.shape[1:], F32))
        for n, offset in enumerate(table):
            if offset in (0, 5, -5) or n == UNITS - 1:
                continue

            @pl.when(u == n)
            def _(offset=offset):
                if abs(offset) in FAR:
                    side = int(offset < 0)
                    node = at(y, zmod(b + (5 if side else -5)))
                    slot = n_recv.at[side, FAR.index(abs(offset))]
                    remote(z_send.at[b], slot, n_s, n_r.at[side], node, head).start()
                else:
                    to_owner(b, offset)

    def gather_far(side):
        b = zmod(z + (-5 if side else 5))
        arrived(y_recv.at[b], ps_r.at[b])
        arrived(n_recv.at[side], n_r.at[side])
        total = n_recv[side, 0].astype(F32)
        for n in range(1, len(FAR)):
            total = total + n_recv[side, n].astype(F32)
        add_up(b, total)
        to_owner(b, -5 if side else 5)

    def pick(u, table):
        value = jnp.int32(table[0])
        for n in range(1, UNITS):
            value = jnp.where(u == n, table[n], value)
        return zmod(z + value)

    def gather_unit(u):
        @pl.when(u != 1)
        def _():
            gather_up(pick(u, FIRST), u, FIRST)
            gather_up(pick(u, SECOND), u, SECOND)

    def unit(u, carry):
        b0, b1 = pick(u, FIRST), pick(u, SECOND)

        @pl.when(jnp.logical_and(u >= 1, u <= 5))
        def _():
            arrived(y_recv.at[b0], qy_r.at[b0])

            @pl.when(u != 2)
            def _():
                arrived(y_recv.at[b1], qy_r.at[b1])

        attend((b0, b1))

        @pl.when(u < UNITS - 1)
        def _():
            hand_out(b0)
            hand_out(b1)

        @pl.when(u == UNITS - 1)
        def _():
            for n, b in enumerate((b0, b1)):
                for d in range(NY):
                    to = ypeer(d)
                    remote(p_send.at[b, to], d_recv.at[n, d], d_s, d_r, at(to, b), head).start()

        @pl.when(u == 0)
        def _():
            for d in (8, 7, -7):
                q_take(d)
            w_relay(2)

        @pl.when(u == 1)
        def _():
            for d in (6, -6, 4, -4):
                q_take(d)
            q_ring(2)

        @pl.when(u == 2)
        def _():
            w_relay(3)

        @pl.when(u == 4)
        def _():
            w_relay(4)

        @pl.when(u == 5)
        def _():
            q_ring(3)

        @pl.when(u == 6)
        def _():
            w_relay(5)

        @pl.when(u >= LAG)
        def _():
            gather_unit(u - LAG)

        return carry

    lax.fori_loop(0, UNITS, unit, 0)
    w_relay(6)

    for side in range(2):
        gather_far(side)
    gather_unit(UNITS - 2)
    w_relay(7)

    arrived(z_recv, z_r)
    arrived(d_recv, d_r)
    total = z_send[z].astype(F32)
    for n in range(len(LAST)):
        for d in range(NY):
            total = total + d_recv[n, d].astype(F32)
    for n in range(len(SLOTS)):
        total = total + z_recv[n].astype(F32)
    a_send[...] = total.astype(BF)
    for d in range(1, NY):
        remote(a_send, a_recv.at[d - 1], a_s, a_r, at(ypeer(d), z), head).start()
        remote(a_send, a_recv.at[NY - 1 + d], a_s, a_r, at(ypeer(d), z), partner).start()
    remote(a_send, a_recv.at[NY - 1], a_s, a_r, seq, partner).start()

    left_here(z_recv.at[:3], qz_s)
    left_here(z_recv.at[:6], qf_s)
    left_here(y_recv.at[:8], qb_s)
    left_here(y_recv.at[:10], qy_s)
    left_here(n_recv, n_s)
    left_here(y_recv.at[: NZ - len(LAST)], ps_s)
    left_here(d_recv, d_s)
    left_here(z_recv, z_s)
    arrived(a_recv, a_r)
    w_relay(8)

    arrived(w_other, wc_r)

    def project(rows, blocks):
        columns = blocks.reshape(wide * w_buf.shape[1], w_buf.shape[2])
        attended = jnp.concatenate(rows, axis=0)
        return lax.dot_general(attended, columns, (((1,), (1,)), ((), ())), preferred_element_type=F32)

    share = project([a_send[...]] + [a_recv[d] for d in range(NY - 1)], w_buf[pl.ds(core * wide, wide)])
    share = share + project([a_recv[NY - 1 + d] for d in range(NY)], w_other[...])
    o_send[...] = share.astype(BF).reshape(o_send.shape)
    for d in range(NY):
        to = lax.rem(y - d + NY, NY)
        copy = remote(o_send.at[d], o_recv.at[x], o_s, o_r, at(to, z), 2 * y + core)
        if d == 0:
            @pl.when(own_out)
            def _():
                pltpu.make_async_copy(o_send.at[0], o_recv.at[x], o_r).start()

            @pl.when(jnp.logical_not(own_out))
            def _():
                copy.start()
        else:
            copy.start()

    left_here(w_other, wc_s)
    left_here(a_recv, a_s)
    left_here(w_buf.at[: NZ - 1], w_s)
    arrived(o_recv, o_r)
    total = o_recv[0].astype(F32)
    for n in range(1, NX):
        total = total + o_recv[n].astype(F32)
    o_ref[...] = total.astype(BF)

    @pl.when(own_out)
    def _():
        left_here(o_recv.at[: NX - 1], o_s)

    @pl.when(jnp.logical_not(own_out))
    def _():
        left_here(o_recv, o_s)


def on_device(queries, keys, values, mask, out_proj):
    width = queries.shape[1]
    block = (ROWS, width)
    dma = pltpu.SemaphoreType.DMA
    return pl.pallas_call(
        kernel,
        out_shape=jax.ShapeDtypeStruct(block, BF),
        in_specs=[pl.BlockSpec(memory_space=pltpu.HBM)] * 5,
        out_specs=pl.BlockSpec(memory_space=pltpu.VMEM),
        scratch_shapes=[
            pltpu.VMEM(mask.shape, mask.dtype),
            pltpu.VMEM((KEYS, 2 * HD), BF),
            pltpu.VMEM((KEYS, HD), BF),
            pltpu.VMEM((8, 8, KEYS), F32),
            pltpu.VMEM((NZ, NY) + block, BF),
            pltpu.VMEM((2 * NY * GROUP * ROWS, 2 * HD), BF),
            pltpu.VMEM((NZ, NY) + block, BF),
            pltpu.VMEM((NZ, NY - 1) + block, BF),
            pltpu.VMEM((NZ,) + block, BF),
            pltpu.VMEM((len(SLOTS),) + block, BF),
            pltpu.VMEM((2, len(FAR)) + block, BF),
            pltpu.VMEM((len(LAST), NY) + block, BF),
            pltpu.VMEM(block, BF),
            pltpu.VMEM((2 * NY - 1,) + block, BF),
            pltpu.VMEM((NZ,) + out_proj.shape[::-1], BF),
            pltpu.VMEM((NZ // 2,) + out_proj.shape[::-1], BF),
            pltpu.VMEM((NY,) + block, BF),
            pltpu.VMEM((NX,) + block, BF),
            dma((6,)),
            dma, dma((NZ,)), dma, dma, dma((NZ,)),
            dma, dma((NZ,)),
            dma, dma((NZ,)),
            dma, dma, dma, dma((2,)), dma, dma,
            dma, dma,
            dma, dma((UNITS + 1,)), dma((UNITS + 1,)),
            dma, dma, dma, dma,
        ],
        compiler_params=pltpu.CompilerParams(
            collective_id=0, has_side_effects=True, vmem_limit_bytes=40 * 1024 * 1024
        ),
        name="attend",
    )(*(pltpu.with_memory_space_constraint(a, pltpu.HBM) for a in (queries, keys, values, mask, out_proj.T)))


def solution(mesh):
    placed = (
        P("seq", "head"),
        P("head", "seq", None),
        P("head", "seq", None),
        P(None, "seq"),
        P("head", "seq"),
    )
    return jax.shard_map(
        on_device, mesh=mesh, in_specs=placed, out_specs=P("seq", "head"), check_vma=False
    )
```
